256 devices in a mesh: gx: 8 (over y, x_hi), gy: 32 (over x_lo, z, core).
Axes of the slice: x: 4 (x_hi: 2, x_lo: 2; x = x_hi * 2 + x_lo), y: 4, z: 8, core: 2. Of those that a mesh axis runs over, the one named last changes fastest.
Arguments:
- draft_in: bfloat16 [64, 16384], P('gy', 'gx')
- verify_in: bfloat16 [256, 16384], P('gy', 'gx')
- accept_len: int32 [64], P('gy'), may hold values from 0 to 3
- norm_gain: bfloat16 [16384], P('gx'), may hold values from 0.099609375 to 1.8984375
- gate_weight: bfloat16 [16384, 28672], P('gx', 'gy'), may hold values from -0.046875 to 0.046875
- up_weight: bfloat16 [16384, 28672], P('gx', 'gy'), may hold values from -0.046875 to 0.046875
- down_weight: bfloat16 [28672, 16384], P('gy', 'gx'), may hold values from -0.03125 to 0.03125
Outputs:
- draft_out: bfloat16 [64, 16384], P('gy', 'gx')
- verify_out: bfloat16 [256, 16384], P('gy', 'gx')
The draws below stay inside these ranges and needn't reach their ends.
All inputs are finite; a program needn't handle non-finite values.
Results may differ from the reference program's by a relative error of at most 0.033.
Values may be sent and summed in bfloat16 or wider, within the bound.
No kernel may reach another device: no remote copies, remote signals or barrier semaphores. Data moves between devices by JAX's collectives and lax.ppermute only.
A program may use at most 64 MiB of HBM per device.

```python
import jax
import jax.numpy as jnp
from jax import lax

D = 16384
FFW = 28672
DRAFT_STEPS = 3
POS = 4
SEQS = 64
N_GX = 8
N_GY = 32


def activations(key, count, row_low, row_high, col_low, col_high):
    value_key, scale_key = jax.random.split(key)
    values = jax.random.normal(value_key, (count, D), jnp.float32)
    row_scale = jnp.exp(jax.random.uniform(scale_key, (count, 1), jnp.float32, jnp.log(row_low), jnp.log(row_high)))
    column = jnp.arange(D, dtype=jnp.float32)[None, :] / (D - 1)
    col_scale = col_low * jnp.exp(column * jnp.log(col_high / col_low))
    return values * row_scale * col_scale


def draw_draft_in(key, part):
    key = jax.random.fold_in(key, 11)
    return activations(key, SEQS, 0.7, 1.5, 0.5, 1.5).astype(jnp.bfloat16)


def draw_verify_in(key, part):
    key = jax.random.fold_in(key, 23)
    return activations(key, SEQS * POS, 0.7, 1.5, 0.5, 1.5).astype(jnp.bfloat16)


def place_ends(result, key, least, high):
    extent = result.shape
    spot = [jax.random.randint(jax.random.fold_in(key, axis), (), 0, extent[axis]) for axis in range(len(extent))]
    result = result.at[tuple(spot)].set(least)
    longest = extent.index(max(extent))
    spot[longest] = (spot[longest] + 1) % extent[longest]
    return result.at[tuple(spot)].set(high)


def block_scale(key, dims, pieces, low, top_value):
    level = 1.0
    for dim, blocks in pieces:
        steps = jax.random.uniform(jax.random.fold_in(jax.random.fold_in(key, 6), dim), (blocks,), jnp.float32, low / len(pieces), top_value / len(pieces))
        level = level * jnp.repeat(jnp.exp(steps), dims[dim] // blocks).reshape((-1,) + (1,) * (len(dims) - 1 - dim))
    return level


def scatter_about(stream_key, shape, spread, limit, shards=(), held_as=jnp.bfloat16):
    drawn = spread * jax.random.normal(stream_key, shape, jnp.float32)
    if shards:
        drawn = drawn * block_scale(stream_key, shape, shards, -0.22, 0.18)
    return jnp.clip(drawn, -limit, limit).astype(held_as)


def setup_inputs(seed: int = 0) -> dict:
    seeds = jax.random.split(jax.random.key(seed), 8)
    return {
        "draft_in": draw_draft_in(jax.random.fold_in(seeds[7], 71), 0),
        "verify_in": draw_verify_in(jax.random.fold_in(seeds[7], 71), 0),
        "accept_len": place_ends(jax.random.randint(seeds[2], (SEQS,), 0, POS), jax.random.fold_in(seeds[2], 1), 0, POS - 1).astype(jnp.int32),
        "norm_gain": jnp.clip(1.0 + 0.18 * jax.random.normal(seeds[3], (D,), jnp.float32), 0.099609375, 1.8984375).astype(jnp.bfloat16),
        "gate_weight": scatter_about(seeds[4], (D, FFW), D ** -0.5, 0.046875, ((0, 8), (1, 32))),
        "up_weight": scatter_about(seeds[5], (D, FFW), D ** -0.5, 0.046875, ((0, 8), (1, 32))),
        "down_weight": scatter_about(seeds[6], (FFW, D), FFW ** -0.5, 0.03125, ((0, 32), (1, 8))),
    }


epsilon = 1e-05

def block_sum(left, weight, parts, round_terms):
    rows = left.shape[0]
    inner = left.shape[1] // parts
    left_blocks = jnp.transpose(left.reshape(rows, parts, inner), (1, 0, 2))
    weight_blocks = weight.reshape(parts, inner, weight.shape[1])

    def add_block(total, pair):
        term = jnp.dot(pair[0].astype(jnp.float32), pair[1].astype(jnp.float32), preferred_element_type=jnp.float32, precision=lax.Precision.HIGHEST)
        if round_terms:
            term = lax.optimization_barrier(term.astype(jnp.bfloat16)).astype(jnp.float32)
        return (total + term, None)
    start_total = jnp.zeros((rows, weight.shape[1]), jnp.float32)
    total, unused = lax.scan(add_block, start_total, (left_blocks, weight_blocks))
    return total

def delta_of(states, norm_gain, gate_weight, up_weight, down_weight):
    float_rows = states.astype(jnp.float32)
    squares = lax.optimization_barrier(jnp.sum(float_rows * float_rows, axis=1, keepdims=True))
    normed = (float_rows * lax.rsqrt(squares / D + epsilon) * norm_gain.astype(jnp.float32)).astype(jnp.bfloat16)
    gate = block_sum(normed, gate_weight, N_GX, True)
    upper = block_sum(normed, up_weight, N_GX, True)
    hidden = (jax.nn.silu(gate) * upper).astype(jnp.bfloat16)
    return block_sum(hidden, down_weight, N_GY, False)

def reference(draft_in, verify_in, accept_len, norm_gain, gate_weight, up_weight, down_weight):
    state = draft_in
    for step in range(DRAFT_STEPS):
        change = delta_of(state, norm_gain, gate_weight, up_weight, down_weight)
        state = (state.astype(jnp.float32) + change).astype(jnp.bfloat16)
    change = delta_of(verify_in, norm_gain, gate_weight, up_weight, down_weight)
    position = jnp.arange(SEQS * POS, dtype=jnp.int32) % POS
    sequence = jnp.arange(SEQS * POS, dtype=jnp.int32) // POS
    live = (position <= accept_len[sequence]).astype(jnp.float32)[:, None]
    verify_out = (verify_in.astype(jnp.float32) + live * change).astype(jnp.bfloat16)
    return (state, verify_out)
```

```python
import jax
import jax.numpy as jnp
from jax import lax
from jax.sharding import Mesh
from jax.sharding import PartitionSpec as P

D = 16384
DRAFT_STEPS = 3
POS = 4
SIZES = {"y": 4, "xh": 2, "xl": 2, "z": 8, "c": 2}
NAMES = tuple(SIZES)
GX = ("y", "xh")
CHIPS = ("xl", "z")
N_GX = 8
N_CHIPS = 16
LANES = 128
epsilon = 1e-05
SHRINK = 2.0**-12


def swap_core(x):
    return lax.ppermute(x, "c", [(0, 1), (1, 0)])


def exchange(x, axes):
    return lax.all_to_all(x, axes, 0, 0)


def spread(x, axes, count):
    return exchange(jnp.broadcast_to(x[None], (count,) + x.shape), axes)


def both_cores(own, core):
    other = swap_core(own)
    first = jnp.where(core == 0, own, other)
    second = jnp.where(core == 0, other, own)
    return jnp.concatenate([first, second], axis=0)


def sum_cores(partial, core):
    half = partial.shape[0] // 2
    low, high = partial[:half], partial[half:]
    other = swap_core(jnp.where(core == 0, high, low))
    own = jnp.where(core == 0, low, high)
    return (own.astype(jnp.float32) + other.astype(jnp.float32)).astype(jnp.bfloat16)


def feed_forward(rows, weights):
    gain, gate_weight, up_weight, down_weight = weights
    count, width = rows.shape
    units = gate_weight.shape[1]
    wide = rows.astype(jnp.float32)
    squares = jnp.sum(wide * wide, axis=1, keepdims=True)
    high = squares.astype(jnp.bfloat16)
    rest = squares - high.astype(jnp.float32)
    low = jnp.where(jnp.isfinite(rest), rest, 0.0).astype(jnp.bfloat16)
    scaled = (wide * (gain.astype(jnp.float32) * SHRINK)).astype(jnp.bfloat16)
    gate = jnp.dot(scaled, gate_weight, preferred_element_type=jnp.float32).astype(jnp.bfloat16)
    up = jnp.dot(scaled, up_weight, preferred_element_type=jnp.float32).astype(jnp.bfloat16)
    lane = lax.broadcasted_iota(jnp.int32, (count, LANES), 1)
    extra = jnp.where(lane == 0, high, jnp.where(lane == 1, low, jnp.zeros_like(high)))
    packet = jnp.concatenate([gate, up, extra], axis=1)
    packet = exchange(packet.reshape(N_GX, count // N_GX, 2 * units + LANES), GX)
    total = jnp.sum(packet.astype(jnp.float32), axis=0)
    sums = total[:, 2 * units : 2 * units + 1] + total[:, 2 * units + 1 : 2 * units + 2]
    scale = lax.rsqrt(sums / D + epsilon) * (1.0 / SHRINK)
    gate = total[:, :units] * scale
    up = total[:, units : 2 * units] * scale
    hidden = (jax.nn.silu(gate) * up).astype(jnp.bfloat16)
    hidden = spread(hidden, GX, N_GX).reshape(count, units)
    return jnp.dot(hidden, down_weight, preferred_element_type=jnp.float32).astype(jnp.bfloat16)


def shards(draft_in, verify_in, accept_len, norm_gain, gate_weight, up_weight, down_weight):
    weights = (norm_gain, gate_weight, up_weight, down_weight)
    core = lax.axis_index("c")
    n_draft, width = draft_in.shape
    n_verify = verify_in.shape[0]
    fold = n_verify // n_draft
    thin = width // fold
    all_draft, all_verify = N_CHIPS * n_draft, N_CHIPS * n_verify

    packet = jnp.concatenate([verify_in, draft_in.reshape(n_verify, thin)], axis=1)
    packet = spread(packet, CHIPS, N_CHIPS)
    own = jnp.concatenate(
        [
            packet[:, :, width:].reshape(all_draft, width),
            packet[:, :, :width].reshape(all_verify, width),
        ],
        axis=0,
    )
    partial = sum_cores(feed_forward(both_cores(own, core), weights), core)
    packet = jnp.concatenate(
        [
            partial[all_draft:].reshape(N_CHIPS, n_verify, width),
            partial[:all_draft].reshape(N_CHIPS, n_verify, thin),
        ],
        axis=2,
    )
    change = jnp.sum(exchange(packet, CHIPS).astype(jnp.float32), axis=0)
    live = (
        (jnp.arange(POS, dtype=jnp.int32)[None, :] <= accept_len[:, None])
        .reshape(-1, 1)
        .astype(jnp.float32)
    )
    verify_out = (verify_in.astype(jnp.float32) + live * change[:, :width]).astype(jnp.bfloat16)
    state = draft_in.astype(jnp.float32) + change[:, width:].reshape(n_draft, width)
    state = state.astype(jnp.bfloat16)

    for step in range(1, DRAFT_STEPS):
        own = spread(state, CHIPS, N_CHIPS).reshape(all_draft, width)
        partial = sum_cores(feed_forward(both_cores(own, core), weights), core)
        packet = exchange(partial.reshape(N_CHIPS, n_draft, width), CHIPS)
        change = jnp.sum(packet.astype(jnp.float32), axis=0)
        state = (state.astype(jnp.float32) + change).astype(jnp.bfloat16)
    return state, verify_out


def solution(mesh):
    split = Mesh(mesh.devices.reshape(tuple(SIZES.values())), NAMES)
    gy = ("xl", "z", "c")
    placed = (P(gy, GX), P(gy, GX), P(gy), P(GX), P(GX, gy), P(GX, gy), P(gy, GX))
    return jax.shard_map(
        shards,
        mesh=split,
        in_specs=placed,
        out_specs=(P(gy, GX), P(gy, GX)),
        check_vma=False,
    )
```

```python
import math

import jax
import jax.numpy as jnp
from jax import lax
from jax.experimental import pallas as pl
from jax.experimental.pallas import tpu as pltpu
from jax.sharding import Mesh
from jax.sharding import PartitionSpec as P

D = 16384
DRAFT_STEPS = 3
POS = 4
SIZES = {"y": 4, "xh": 2, "xl": 2, "z": 8, "c": 2}
NAMES = tuple(SIZES)
GX = ("y", "xh")
CHIPS = ("xl", "z")
N_GX = 8
N_CHIPS = 16
LANES = 128
LOAD = 32 << 20
epsilon = 1e-05
SHRINK = 2.0**-12


def swap(x, axis, distance):
    return lax.ppermute(x, axis, [(i, i ^ distance) for i in range(SIZES[axis])])


def exchange(x, axes):
    return lax.all_to_all(x, axes, 0, 0)


def repeat_kernel(x, out):
    values = x[...]
    for i in range(out.shape[0]):
        out[i] = values


def stack_kernel(first, second, out):
    count = first.shape[0]
    out[:count] = first[...]
    out[count:] = second[...]


def packet_kernel(verify, draft, out):
    width, thin = verify.shape[1], out.shape[2] - verify.shape[1]
    rows = draft[...].astype(jnp.float32)
    folded = [
        rows[r : r + 1, k * thin : (k + 1) * thin]
        for r in range(rows.shape[0])
        for k in range(width // thin)
    ]
    folded = jnp.concatenate(folded, axis=0).astype(out.dtype)
    values = verify[...]
    for i in range(out.shape[0]):
        out[i, :, :width] = values
        out[i, :, width:] = folded


def columns_kernel(blocks, out):
    size = blocks.shape[2]
    for k in range(blocks.shape[0]):
        out[:, k * size : (k + 1) * size] = blocks[k]


def rearrange(kernel, arrays, shape, name, load=0):
    vmem = pl.BlockSpec(memory_space=pltpu.VMEM)
    return pl.pallas_call(
        kernel,
        out_shape=jax.ShapeDtypeStruct(shape, jnp.bfloat16),
        in_specs=[vmem] * len(arrays),
        out_specs=vmem,
        compiler_params=pltpu.CompilerParams(vmem_limit_bytes=8 << 20),
        cost_estimate=pl.CostEstimate(
            flops=load * 600, bytes_accessed=4 * math.prod(shape) + load, transcendentals=0
        ),
        name=name,
    )(*arrays)


def spread(x, axes, count):
    copies = rearrange(repeat_kernel, (x,), (count,) + x.shape, "repeat", LOAD)
    return exchange(copies, axes)


def wide(x):
    return x.astype(jnp.float32)


def narrow(x):
    return x.astype(jnp.bfloat16)


def pair(own, axis, distance):
    return jnp.concatenate([own, swap(own, axis, distance)], axis=0)


def halves(rows, upper=None):
    half = rows.shape[0] // 2
    low, high = rows[:half], rows[half:]
    if upper is None:
        return low, high
    return jnp.where(upper, high, low), jnp.where(upper, low, high)


def columns(blocks):
    count, rows, lanes = blocks.shape
    return rearrange(columns_kernel, (blocks,), (rows, count * lanes), "columns")


def blocks_of(x, count):
    return jnp.transpose(x.reshape(x.shape[0], count, -1), (1, 0, 2))


def summed(packet):
    return jnp.sum(wide(packet), axis=0)


def up_product(rows, gain, marks, weights):
    gate_weight, up_weight = weights[:2]
    values = wide(rows)
    squares = jnp.sum(values * values, axis=1, keepdims=True)
    high = narrow(squares)
    rest = squares - wide(high)
    low = narrow(jnp.where(jnp.isfinite(rest), rest, 0.0))
    scaled = narrow(values * gain)
    gate = narrow(jnp.dot(scaled, gate_weight, preferred_element_type=jnp.float32))
    up = narrow(jnp.dot(scaled, up_weight, preferred_element_type=jnp.float32))
    first, second = marks
    extra = jnp.where(first, high, jnp.where(second, low, jnp.zeros_like(high)))
    return jnp.concatenate([gate, up, extra], axis=1)


def activate(total):
    units = (total.shape[1] - LANES) // 2
    sums = total[:, 2 * units : 2 * units + 1] + total[:, 2 * units + 1 : 2 * units + 2]
    scale = lax.rsqrt(sums / D + epsilon) * (1.0 / SHRINK)
    gate = total[:, :units] * scale
    up = total[:, units : 2 * units] * scale
    return narrow(jax.nn.silu(gate) * up)


def down_product(hidden, weights):
    return narrow(jnp.dot(hidden, weights[2], preferred_element_type=jnp.float32))


def shards(draft_in, verify_in, accept_len, norm_gain, gate_weight, up_weight, down_weight):
    weights = (gate_weight, up_weight, down_weight)
    n_draft, width = draft_in.shape
    n_verify = verify_in.shape[0]
    units = gate_weight.shape[1]
    thin = n_draft * width // n_verify
    all_draft, all_verify = N_CHIPS * n_draft, N_CHIPS * n_verify
    y, x_low, z = lax.axis_index("y"), lax.axis_index("xl"), lax.axis_index("z")
    near, across, far = y % 2 == 1, lax.axis_index("xh") == 1, y // 2 == 1
    chip = x_low * SIZES["z"] + z
    near, column = lax.optimization_barrier((near, chip * LANES))
    mine = (lax.broadcasted_iota(jnp.int32, (1, width), 1) // LANES) == chip
    always = accept_len[0] >= 0

    def part(body, *operands):
        def empty(*rest):
            return jax.tree.map(
                lambda a: jnp.zeros(a.shape, a.dtype), jax.eval_shape(body, *rest)
            )

        return lax.cond(always, body, empty, *operands)

    def beside(send, axis, distance, body, *operands):
        send, operands = lax.optimization_barrier((send, operands))
        arrived = swap(send, axis, distance)
        result = part(body, *operands)
        return lax.optimization_barrier((arrived, result))

    def add(keep, arrived):
        return wide(keep) + wide(arrived)

    def first_rows(draft, verify, gain):
        shape = (N_CHIPS, n_verify, width + thin)
        packet = exchange(rearrange(packet_kernel, (verify, draft), shape, "packet"), CHIPS)
        draft = packet[:, :, width:].reshape(all_draft, width)
        verify = packet[:, :, :width].reshape(all_verify, width)
        shape = (all_draft + all_verify, width)
        rows = pair(rearrange(stack_kernel, (draft, verify), shape, "stack", LOAD), "c", 1)
        gain = wide(gain) * SHRINK
        lane = lax.broadcasted_iota(jnp.int32, (1, LANES), 1)
        marks = lane == 0, lane == 1
        low, high = halves(up_product(rows, gain, marks, weights))
        keep = jnp.where(near, high[all_draft:], low[all_draft:])
        send = jnp.where(near, low[all_draft:], high[all_draft:])
        state = lax.dynamic_slice(
            draft, (0, column), (all_draft, LANES), allow_negative_indices=False
        )
        packet = jnp.concatenate([low[:all_draft], high[:all_draft]], axis=0)
        return packet, state, keep, send, gain, marks

    def rows_in(state, gain, marks):
        own = columns(spread(state, CHIPS, N_CHIPS))
        return up_product(pair(own, "c", 1), gain, marks, weights)

    def sum_width(packet):
        packet = packet.reshape(N_GX, -1, packet.shape[1])
        return activate(summed(exchange(packet, GX)))

    def share_hidden(hidden):
        hidden = spread(hidden, GX, N_GX).reshape(-1, units)
        keep, send = halves(down_product(hidden, weights))
        return narrow(add(keep, swap(send, "c", 1)))

    def share_last(hidden, state):
        hidden = spread(hidden, GX, N_GX).reshape(-1, units)
        keep, send = halves(down_product(hidden, weights))
        total = add(keep, swap(send, "c", 1))
        return narrow(total + jnp.where(mine, jnp.tile(wide(state), (1, N_CHIPS)), 0.0))

    def share_both(hidden, verify):
        n_own = hidden.shape[0]
        both = spread(jnp.concatenate([hidden, verify], axis=0), GX, N_GX)
        hidden = both[:, :n_own].reshape(-1, units)
        verify = both[:, n_own:].reshape(2, 2, 2, 2, 2, n_verify, units)
        verify = jnp.transpose(verify, (1, 2, 4, 3, 0, 5, 6)).reshape(2, all_verify, units)
        half = all_draft
        rows = [hidden[:half], verify[0], hidden[half:], verify[1]]
        keep, send = halves(down_product(jnp.concatenate(rows, axis=0), weights))
        total = narrow(add(keep, swap(send, "c", 1)))
        return total[:half], total[half:]

    def sum_units(partial, state):
        change = summed(exchange(blocks_of(partial, N_CHIPS), CHIPS))
        return narrow(wide(state) + change)

    def last_sum(partial):
        return narrow(summed(exchange(partial.reshape(N_CHIPS, n_draft, width), CHIPS)))

    packet, state, keep, send, gain, marks = part(first_rows, draft_in, verify_in, norm_gain)
    hidden = part(sum_width, packet)
    arrived, partial = beside(send, "y", 1, share_hidden, hidden)
    keep, send = halves(narrow(add(keep, arrived)), across)
    arrived, state = beside(send, "xh", 1, sum_units, partial, state)
    keep, send = halves(narrow(add(keep, arrived)), far)
    arrived, packet = beside(send, "y", 2, rows_in, state, gain, marks)
    verify = activate(add(keep, arrived))
    hidden = part(sum_width, packet)
    partial, verify = part(share_both, hidden, verify)
    keep, send = halves(verify, x_low == 1)
    arrived, state = beside(send, "xl", 1, sum_units, partial, state)
    keep, send = halves(narrow(add(keep, arrived)), z % 2 == 1)
    arrived, packet = beside(send, "z", 1, rows_in, state, gain, marks)
    keep, send = halves(narrow(add(keep, arrived)), z // 2 % 2 == 1)
    arrived, hidden = beside(send, "z", 2, sum_width, packet)
    keep, send = halves(narrow(add(keep, arrived)), z // 4 == 1)
    arrived, partial = beside(send, "z", 4, share_last, hidden, state)
    live = (
        (jnp.arange(POS, dtype=jnp.int32)[None, :] <= accept_len[:, None])
        .reshape(-1, 1)
        .astype(jnp.float32)
    )
    verify_out = narrow(wide(verify_in) + live * add(keep, arrived))
    draft_out = part(last_sum, partial)
    return draft_out, verify_out


def solution(mesh):
    split = Mesh(mesh.devices.reshape(tuple(SIZES.values())), NAMES)
    gy = ("xl", "z", "c")
    placed = (P(gy, GX), P(gy, GX), P(gy), P(GX), P(GX, gy), P(GX, gy), P(gy, GX))
    return jax.shard_map(
        shards,
        mesh=split,
        in_specs=placed,
        out_specs=(P(gy, GX), P(gy, GX)),
        check_vma=False,
    )
```

```python
import math

import jax
import jax.numpy as jnp
from jax import lax
from jax.experimental import pallas as pl
from jax.experimental.pallas import tpu as pltpu
from jax.sharding import Mesh
from jax.sharding import PartitionSpec as P

D = 16384
DRAFT_STEPS = 3
POS = 4
SIZES = {"y": 4, "xh": 2, "xl": 2, "z": 8, "c": 2}
NAMES = tuple(SIZES)
GX = ("y", "xh")
CHIPS = ("xl", "z")
N_GX = 8
N_CHIPS = 16
LANES = 128
LOAD = 32 << 20
epsilon = 1e-05
SHRINK = 2.0**-12


def swap(x, axis, distance):
    return lax.ppermute(x, axis, [(i, i ^ distance) for i in range(SIZES[axis])])


def exchange(x, axes):
    return lax.all_to_all(x, axes, 0, 0)


def repeat_kernel(x, out):
    values = x[...]
    for i in range(out.shape[0]):
        out[i] = values


def stack_kernel(first, second, out):
    count = first.shape[0]
    out[:count] = first[...]
    out[count:] = second[...]


def packet_kernel(verify, draft, out):
    width, thin = verify.shape[1], out.shape[2] - verify.shape[1]
    rows = draft[...].astype(jnp.float32)
    folded = [
        rows[r : r + 1, k * thin : (k + 1) * thin]
        for r in range(rows.shape[0])
        for k in range(width // thin)
    ]
    folded = jnp.concatenate(folded, axis=0).astype(out.dtype)
    values = verify[...]
    for i in range(out.shape[0]):
        out[i, :, :width] = values
        out[i, :, width:] = folded


def columns_kernel(blocks, out):
    size = blocks.shape[2]
    for k in range(blocks.shape[0]):
        out[:, k * size : (k + 1) * size] = blocks[k]


def rearrange(kernel, arrays, shape, name, load=0):
    vmem = pl.BlockSpec(memory_space=pltpu.VMEM)
    return pl.pallas_call(
        kernel,
        out_shape=jax.ShapeDtypeStruct(shape, jnp.bfloat16),
        in_specs=[vmem] * len(arrays),
        out_specs=vmem,
        compiler_params=pltpu.CompilerParams(vmem_limit_bytes=8 << 20),
        cost_estimate=pl.CostEstimate(
            flops=load * 600, bytes_accessed=4 * math.prod(shape) + load, transcendentals=0
        ),
        name=name,
    )(*arrays)


def spread(x, axes, count):
    copies = rearrange(repeat_kernel, (x,), (count,) + x.shape, "repeat", LOAD)
    return exchange(copies, axes)


def wide(x):
    return x.astype(jnp.float32)


def narrow(x):
    return x.astype(jnp.bfloat16)


def pair(own, axis, distance):
    return jnp.concatenate([own, swap(own, axis, distance)], axis=0)


def halves(rows, upper=None):
    half = rows.shape[0] // 2
    low, high = rows[:half], rows[half:]
    if upper is None:
        return low, high
    return jnp.where(upper, high, low), jnp.where(upper, low, high)


def columns(blocks):
    count, rows, lanes = blocks.shape
    return rearrange(columns_kernel, (blocks,), (rows, count * lanes), "columns")


def blocks_of(x, count):
    return jnp.transpose(x.reshape(x.shape[0], count, -1), (1, 0, 2))


def summed(packet):
    return jnp.sum(wide(packet), axis=0)


def up_product(rows, gain, marks, weights):
    gate_weight, up_weight = weights[:2]
    values = wide(rows)
    squares = jnp.sum(values * values, axis=1, keepdims=True)
    high = narrow(squares)
    rest = squares - wide(high)
    low = narrow(jnp.where(jnp.isfinite(rest), rest, 0.0))
    scaled = narrow(values * SHRINK * wide(gain))
    gate = narrow(jnp.dot(scaled, gate_weight, preferred_element_type=jnp.float32))
    up = narrow(jnp.dot(scaled, up_weight, preferred_element_type=jnp.float32))
    first, second = marks
    extra = jnp.where(first, high, jnp.where(second, low, jnp.zeros_like(high)))
    return jnp.concatenate([gate, up, extra], axis=1)


def activate(total):
    units = (total.shape[1] - LANES) // 2
    sums = total[:, 2 * units : 2 * units + 1] + total[:, 2 * units + 1 : 2 * units + 2]
    scale = lax.rsqrt(sums / D + epsilon) * (1.0 / SHRINK)
    gate = total[:, :units] * scale
    up = total[:, units : 2 * units] * scale
    return narrow(jax.nn.silu(gate) * up)


def down_product(hidden, weights):
    return narrow(jnp.dot(hidden, weights[2], preferred_element_type=jnp.float32))


def shards(draft_in, verify_in, accept_len, norm_gain, gate_weight, up_weight, down_weight):
    weights = (gate_weight, up_weight, down_weight)
    n_draft, width = draft_in.shape
    n_verify = verify_in.shape[0]
    units = gate_weight.shape[1]
    thin = n_draft * width // n_verify
    all_draft, all_verify = N_CHIPS * n_draft, N_CHIPS * n_verify
    y, x_low, z = lax.axis_index("y"), lax.axis_index("xl"), lax.axis_index("z")
    near, across, far = y % 2 == 1, lax.axis_index("xh") == 1, y // 2 == 1
    chip = x_low * SIZES["z"] + z
    near, column = lax.optimization_barrier((near, chip * LANES))
    mine = (lax.broadcasted_iota(jnp.int32, (1, width), 1) // LANES) == chip
    always = accept_len[0] >= 0

    def part(body, *operands):
        def empty(*rest):
            return jax.tree.map(
                lambda a: jnp.zeros(a.shape, a.dtype), jax.eval_shape(body, *rest)
            )

        return lax.cond(always, body, empty, *operands)

    def beside(send, axis, distance, body, *operands):
        send, operands = lax.optimization_barrier((send, operands))
        arrived = swap(send, axis, distance)
        result = part(body, *operands)
        return lax.optimization_barrier((arrived, result))

    def add(keep, arrived):
        return wide(keep) + wide(arrived)

    def first_rows(draft, verify, gain):
        shape = (N_CHIPS, n_verify, width + thin)
        packet = exchange(rearrange(packet_kernel, (verify, draft), shape, "packet"), CHIPS)
        draft = packet[:, :, width:].reshape(all_draft, width)
        verify = packet[:, :, :width].reshape(all_verify, width)
        shape = (all_draft + all_verify, width)
        rows = pair(rearrange(stack_kernel, (draft, verify), shape, "stack", LOAD), "c", 1)
        lane = lax.broadcasted_iota(jnp.int32, (1, LANES), 1)
        marks = lane == 0, lane == 1
        low, high = halves(up_product(rows, gain, marks, weights))
        keep = jnp.where(near, high[all_draft:], low[all_draft:])
        send = jnp.where(near, low[all_draft:], high[all_draft:])
        state = lax.dynamic_slice(
            draft, (0, column), (all_draft, LANES), allow_negative_indices=False
        )
        packet = jnp.concatenate([low[:all_draft], high[:all_draft]], axis=0)
        return packet, state, keep, send, marks

    def rows_in(state, gain, marks):
        own = columns(spread(state, CHIPS, N_CHIPS))
        return up_product(pair(own, "c", 1), gain, marks, weights)

    def sum_width(packet):
        packet = packet.reshape(N_GX, -1, packet.shape[1])
        return activate(summed(exchange(packet, GX)))

    def share_hidden(hidden):
        hidden = spread(hidden, GX, N_GX).reshape(-1, units)
        keep, send = halves(down_product(hidden, weights))
        return narrow(add(keep, swap(send, "c", 1)))

    def share_last(hidden, state):
        hidden = spread(hidden, GX, N_GX).reshape(-1, units)
        keep, send = halves(down_product(hidden, weights))
        total = add(keep, swap(send, "c", 1))
        return narrow(total + jnp.where(mine, jnp.tile(wide(state), (1, N_CHIPS)), 0.0))

    def share_both(hidden, verify):
        n_own = hidden.shape[0]
        both = spread(jnp.concatenate([hidden, verify], axis=0), GX, N_GX)
        hidden = both[:, :n_own].reshape(-1, units)
        verify = both[:, n_own:].reshape(2, 2, 2, 2, 2, n_verify, units)
        verify = jnp.transpose(verify, (1, 2, 4, 3, 0, 5, 6)).reshape(2, all_verify, units)
        half = all_draft
        rows = [hidden[:half], verify[0], hidden[half:], verify[1]]
        keep, send = halves(down_product(jnp.concatenate(rows, axis=0), weights))
        total = narrow(add(keep, swap(send, "c", 1)))
        return total[:half], total[half:]

    def sum_units(partial, state):
        change = summed(exchange(blocks_of(partial, N_CHIPS), CHIPS))
        return narrow(wide(state) + change)

    def last_sum(partial):
        return narrow(summed(exchange(partial.reshape(N_CHIPS, n_draft, width), CHIPS)))

    packet, state, keep, send, marks = part(first_rows, draft_in, verify_in, norm_gain)
    hidden = part(sum_width, packet)
    partial = part(share_hidden, hidden)
    arrived, state = beside(send, "y", 1, sum_units, partial, state)
    keep, send = halves(narrow(add(keep, arrived)), across)
    arrived, packet = beside(send, "xh", 1, rows_in, state, norm_gain, marks)
    keep, send = halves(narrow(add(keep, arrived)), far)
    arrived, hidden = beside(send, "y", 2, sum_width, packet)
    verify = activate(add(keep, arrived))
    partial, verify = part(share_both, hidden, verify)
    keep, send = halves(verify, x_low == 1)
    arrived, state = beside(send, "xl", 1, sum_units, partial, state)
    keep, send = halves(narrow(add(keep, arrived)), z % 2 == 1)
    arrived, packet = beside(send, "z", 1, rows_in, state, norm_gain, marks)
    keep, send = halves(narrow(add(keep, arrived)), z // 2 % 2 == 1)
    arrived, hidden = beside(send, "z", 2, sum_width, packet)
    keep, send = halves(narrow(add(keep, arrived)), z // 4 == 1)
    arrived, partial = beside(send, "z", 4, share_last, hidden, state)
    live = (
        (jnp.arange(POS, dtype=jnp.int32)[None, :] <= accept_len[:, None])
        .reshape(-1, 1)
        .astype(jnp.float32)
    )
    verify_out = narrow(wide(verify_in) + live * add(keep, arrived))
    draft_out = part(last_sum, partial)
    return draft_out, verify_out


def solution(mesh):
    split = Mesh(mesh.devices.reshape(tuple(SIZES.values())), NAMES)
    gy = ("xl", "z", "c")
    placed = (P(gy, GX), P(gy, GX), P(gy), P(GX), P(GX, gy), P(GX, gy), P(gy, GX))
    return jax.shard_map(
        shards,
        mesh=split,
        in_specs=placed,
        out_specs=(P(gy, GX), P(gy, GX)),
        check_vma=False,
    )
```

```python
import math

import jax
import jax.numpy as jnp
from jax import lax
from jax.experimental import pallas as pl
from jax.experimental.pallas import tpu as pltpu
from jax.sharding import Mesh
from jax.sharding import PartitionSpec as P

D = 16384
DRAFT_STEPS = 3
POS = 4
SIZES = {"y": 4, "xh": 2, "xl": 2, "z": 8, "c": 2}
NAMES = tuple(SIZES)
GX = ("y", "xh")
CHIPS = ("xl", "z")
N_GX = 8
N_CHIPS = 16
LANES = 128
LOAD = 32 << 20
epsilon = 1e-05
SHRINK = 2.0**-12


def swap(x, axes, distance):
    count = math.prod(SIZES[axis] for axis in ([axes] if isinstance(axes, str) else axes))
    return lax.ppermute(x, axes, [(i, i ^ distance) for i in range(count)])


def exchange(x, axes):
    return lax.all_to_all(x, axes, 0, 0)


def repeat_kernel(x, out):
    values = x[...]
    for i in range(out.shape[0]):
        out[i] = values


def stack_kernel(*refs):
    rows = [ref[...].astype(jnp.float32) for ref in refs[:-1]]
    refs[-1][...] = jnp.concatenate(rows, axis=0).astype(refs[-1].dtype)


def copy_kernel(x, out):
    out[...] = x[...]


def columns_kernel(blocks, out):
    size = blocks.shape[2]
    for k in range(blocks.shape[0]):
        out[:, k * size : (k + 1) * size] = blocks[k]


def rearrange(kernel, arrays, shape, name, load=0):
    vmem = pl.BlockSpec(memory_space=pltpu.VMEM)
    return pl.pallas_call(
        kernel,
        out_shape=jax.ShapeDtypeStruct(shape, jnp.bfloat16),
        in_specs=[vmem] * len(arrays),
        out_specs=vmem,
        compiler_params=pltpu.CompilerParams(vmem_limit_bytes=8 << 20),
        cost_estimate=pl.CostEstimate(
            flops=load * 600, bytes_accessed=4 * math.prod(shape) + load, transcendentals=0
        ),
        name=name,
    )(*arrays)


def stack(*arrays):
    count, width = arrays[0].shape
    return rearrange(stack_kernel, arrays, (len(arrays) * count, width), "stack")


def spread(x, axes, count):
    copies = rearrange(repeat_kernel, (x,), (count,) + x.shape, "repeat", LOAD)
    return exchange(copies, axes)


def wide(x):
    return x.astype(jnp.float32)


def narrow(x):
    return x.astype(jnp.bfloat16)


def pair(own, axis, distance):
    return jnp.concatenate([own, swap(own, axis, distance)], axis=0)


def halves(rows, upper=None):
    half = rows.shape[0] // 2
    low, high = rows[:half], rows[half:]
    if upper is None:
        return low, high
    return jnp.where(upper, high, low), jnp.where(upper, low, high)


def columns(blocks):
    count, rows, lanes = blocks.shape
    return rearrange(columns_kernel, (blocks,), (rows, count * lanes), "columns")


def blocks_of(x, count):
    return jnp.transpose(x.reshape(x.shape[0], count, -1), (1, 0, 2))


def summed(packet):
    return jnp.sum(wide(packet), axis=0)


def up_product(rows, gain, marks, weights):
    gate_weight, up_weight = weights[:2]
    values = wide(rows)
    squares = jnp.sum(values * values, axis=1, keepdims=True)
    high = narrow(squares)
    rest = squares - wide(high)
    low = narrow(jnp.where(jnp.isfinite(rest), rest, 0.0))
    scaled = narrow(values * SHRINK * wide(gain))
    gate = narrow(jnp.dot(scaled, gate_weight, preferred_element_type=jnp.float32))
    up = narrow(jnp.dot(scaled, up_weight, preferred_element_type=jnp.float32))
    first, second = marks
    extra = jnp.where(first, high, jnp.where(second, low, jnp.zeros_like(high)))
    return jnp.concatenate([gate, up, extra], axis=1)


def activate(total):
    units = (total.shape[1] - LANES) // 2
    sums = total[:, 2 * units : 2 * units + 1] + total[:, 2 * units + 1 : 2 * units + 2]
    scale = lax.rsqrt(sums / D + epsilon) * (1.0 / SHRINK)
    gate = total[:, :units] * scale
    up = total[:, units : 2 * units] * scale
    return narrow(jax.nn.silu(gate) * up)


def down_product(hidden, weights):
    return narrow(jnp.dot(hidden, weights[2], preferred_element_type=jnp.float32))


def shards(draft_in, verify_in, accept_len, norm_gain, gate_weight, up_weight, down_weight):
    weights = (gate_weight, up_weight, down_weight)
    n_draft, width = draft_in.shape
    n_verify = verify_in.shape[0]
    units = gate_weight.shape[1]
    all_draft = N_CHIPS * n_draft
    y = lax.axis_index("y")
    near, across, far = y % 2 == 1, lax.axis_index("xh") == 1, y // 2 == 1
    chip = lax.axis_index("xl") * SIZES["z"] + lax.axis_index("z")
    lane = lax.broadcasted_iota(jnp.int32, (1, LANES), 1)
    near, column, lane = lax.optimization_barrier((near, chip * LANES, lane))
    marks = lane == 0, lane == 1
    mine = (lax.broadcasted_iota(jnp.int32, (1, width), 1) // LANES) == chip
    always = accept_len[0] >= 0

    def part(body, *operands):
        def empty(*rest):
            return jax.tree.map(
                lambda a: jnp.zeros(a.shape, a.dtype), jax.eval_shape(body, *rest)
            )

        return lax.cond(always, body, empty, *operands)

    def beside(send, swaps, body, *operands):
        send, operands = lax.optimization_barrier((send, operands))
        arrived = [swap(send, axes, distance) for axes, distance in swaps]
        result = part(body, *operands)
        return lax.optimization_barrier((*arrived, result))

    def add(keep, arrived):
        return wide(keep) + wide(arrived)

    def first_rows(draft, gain, marks):
        draft = spread(draft, CHIPS, N_CHIPS)
        draft, gain = lax.optimization_barrier((draft, gain))
        draft = draft.reshape(all_draft, width)
        own = rearrange(copy_kernel, (draft,), draft.shape, "own", LOAD)
        start = (0, column)
        state = lax.dynamic_slice(
            draft, start, (all_draft, LANES), allow_negative_indices=False
        )
        return up_product(pair(own, "c", 1), gain, marks, weights), state

    def rows_in(state, gain, marks):
        own = columns(spread(state, CHIPS, N_CHIPS))
        return up_product(pair(own, "c", 1), gain, marks, weights)

    def sum_width(packet):
        packet = packet.reshape(N_GX, -1, packet.shape[1])
        return activate(summed(exchange(packet, GX)))

    def share_hidden(hidden):
        hidden = spread(hidden, GX, N_GX).reshape(-1, units)
        keep, send = halves(down_product(hidden, weights))
        return narrow(add(keep, swap(send, "c", 1)))

    def share_first(hidden, verify, gain, marks):
        hidden = spread(hidden, GX, N_GX).reshape(-1, units)
        hidden, verify, gain = lax.optimization_barrier((hidden, verify, gain))
        keep, send = halves(down_product(hidden, weights))
        partial = narrow(add(keep, swap(send, "c", 1)))
        own = up_product(verify, gain, marks, weights)
        other = up_product(swap(verify, "c", 1), gain, marks, weights)
        return partial, jnp.where(near, other, own), jnp.where(near, own, other)

    def share_both(hidden, verify):
        n_own = hidden.shape[0]
        both = spread(jnp.concatenate([hidden, verify], axis=0), GX, N_GX)
        hidden = both[:, :n_own].reshape(-1, units)
        keep, send = halves(down_product(hidden, weights))
        partial = narrow(add(keep, swap(send, "c", 1)))
        verify = both[:, n_own:].reshape(2, 2, 2, 2, 2, n_verify, units)
        verify = jnp.transpose(verify, (1, 2, 0, 4, 3, 5, 6)).reshape(-1, units)
        return partial, *halves(down_product(verify, weights))

    def share_last(hidden, state):
        hidden = spread(hidden, GX, N_GX).reshape(-1, units)
        keep, send = halves(down_product(hidden, weights))
        total = add(keep, swap(send, "c", 1))
        return narrow(total + jnp.where(mine, jnp.tile(wide(state), (1, N_CHIPS)), 0.0))

    def sum_units(partial, state):
        change = summed(exchange(blocks_of(partial, N_CHIPS), CHIPS))
        return narrow(wide(state) + change)

    def last_sum(partial):
        return narrow(summed(exchange(partial.reshape(N_CHIPS, n_draft, width), CHIPS)))

    swaps = [("z", 4), ("z", 2), ("z", 6)]
    far_z, near_z, both_z, (packet, state) = beside(
        verify_in, swaps, first_rows, draft_in, norm_gain, marks
    )
    verify = stack(verify_in, near_z, far_z, both_z)
    swaps = [(CHIPS, 1), (CHIPS, 8), (CHIPS, 9)]
    near_z, low_x, both, hidden = beside(verify, swaps, sum_width, packet)
    verify = stack(verify, near_z, low_x, both)
    partial, keep, send = part(share_first, hidden, verify, norm_gain, marks)
    arrived, state = beside(send, [("y", 1)], sum_units, partial, state)
    keep, send = halves(narrow(add(keep, arrived)), across)
    arrived, packet = beside(send, [("xh", 1)], rows_in, state, norm_gain, marks)
    keep, send = halves(narrow(add(keep, arrived)), far)
    arrived, hidden = beside(send, [("y", 2)], sum_width, packet)
    verify = activate(add(keep, arrived))
    partial, keep, send = part(share_both, hidden, verify)
    arrived, state = beside(send, [("c", 1)], sum_units, partial, state)
    keep, send = halves(narrow(add(keep, arrived)))
    arrived, packet = beside(send, [("xl", 1)], rows_in, state, norm_gain, marks)
    keep, send = halves(narrow(add(keep, arrived)))
    arrived, hidden = beside(send, [("z", 1)], sum_width, packet)
    keep, send = halves(narrow(add(keep, arrived)))
    arrived, partial = beside(send, [("z", 2)], share_last, hidden, state)
    keep, send = halves(narrow(add(keep, arrived)))
    arrived, draft_out = beside(send, [("z", 4)], last_sum, partial)
    live = (
        (jnp.arange(POS, dtype=jnp.int32)[None, :] <= accept_len[:, None])
        .reshape(-1, 1)
        .astype(jnp.float32)
    )
    verify_out = narrow(wide(verify_in) + live * add(keep, arrived))
    return draft_out, verify_out


def solution(mesh):
    split = Mesh(mesh.devices.reshape(tuple(SIZES.values())), NAMES)
    gy = ("xl", "z", "c")
    placed = (P(gy, GX), P(gy, GX), P(gy), P(GX), P(GX, gy), P(GX, gy), P(gy, GX))
    return jax.shard_map(
        shards,
        mesh=split,
        in_specs=placed,
        out_specs=(P(gy, GX), P(gy, GX)),
        check_vma=False,
    )
```

```python
import math

import jax
import jax.numpy as jnp
from jax import lax
from jax.experimental import pallas as pl
from jax.experimental.pallas import tpu as pltpu
from jax.sharding import Mesh
from jax.sharding import PartitionSpec as P

D = 16384
DRAFT_STEPS = 3
POS = 4
SIZES = {"y": 4, "xh": 2, "xl": 2, "z": 8, "c": 2}
NAMES = tuple(SIZES)
GX = ("y", "xh")
CHIPS = ("xl", "z")
N_GX = 8
N_CHIPS = 16
LANES = 128
LOAD = 32 << 20
epsilon = 1e-05
SHRINK = 2.0**-12


def swap(x, axes, distance):
    count = math.prod(SIZES[axis] for axis in ([axes] if isinstance(axes, str) else axes))
    return lax.ppermute(x, axes, [(i, i ^ distance) for i in range(count)])


def exchange(x, axes):
    return lax.all_to_all(x, axes, 0, 0)


def repeat_kernel(x, out):
    values = x[...]
    for i in range(out.shape[0]):
        out[i] = values


def stack_kernel(*refs):
    rows = [ref[...].astype(jnp.float32) for ref in refs[:-1]]
    refs[-1][...] = jnp.concatenate(rows, axis=0).astype(refs[-1].dtype)


def copy_kernel(x, out):
    out[...] = x[...]


def columns_kernel(blocks, out):
    size = blocks.shape[2]
    for k in range(blocks.shape[0]):
        out[:, k * size : (k + 1) * size] = blocks[k]


def rearrange(kernel, arrays, shape, name, load=0):
    vmem = pl.BlockSpec(memory_space=pltpu.VMEM)
    return pl.pallas_call(
        kernel,
        out_shape=jax.ShapeDtypeStruct(shape, jnp.bfloat16),
        in_specs=[vmem] * len(arrays),
        out_specs=vmem,
        compiler_params=pltpu.CompilerParams(vmem_limit_bytes=8 << 20),
        cost_estimate=pl.CostEstimate(
            flops=load * 600, bytes_accessed=4 * math.prod(shape) + load, transcendentals=0
        ),
        name=name,
    )(*arrays)


def stack(*arrays):
    count, width = arrays[0].shape
    return rearrange(stack_kernel, arrays, (len(arrays) * count, width), "stack")


def spread(x, axes, count):
    copies = rearrange(repeat_kernel, (x,), (count,) + x.shape, "repeat", LOAD)
    return exchange(copies, axes)


def wide(x):
    return x.astype(jnp.float32)


def narrow(x):
    return x.astype(jnp.bfloat16)


def pair(own, axis, distance):
    return jnp.concatenate([own, swap(own, axis, distance)], axis=0)


def halves(rows, upper=None):
    half = rows.shape[0] // 2
    low, high = rows[:half], rows[half:]
    if upper is None:
        return low, high
    return jnp.where(upper, high, low), jnp.where(upper, low, high)


def columns(blocks):
    count, rows, lanes = blocks.shape
    return rearrange(columns_kernel, (blocks,), (rows, count * lanes), "columns")


def blocks_of(x, count):
    return jnp.transpose(x.reshape(x.shape[0], count, -1), (1, 0, 2))


def summed(packet):
    return jnp.sum(wide(packet), axis=0)


def up_product(rows, gain, marks, weights):
    gate_weight, up_weight = weights[:2]
    values = wide(rows)
    squares = jnp.sum(values * values, axis=1, keepdims=True)
    high = narrow(squares)
    rest = squares - wide(high)
    low = narrow(jnp.where(jnp.isfinite(rest), rest, 0.0))
    scaled = narrow(values * SHRINK * wide(gain))
    gate = narrow(jnp.dot(scaled, gate_weight, preferred_element_type=jnp.float32))
    up = narrow(jnp.dot(scaled, up_weight, preferred_element_type=jnp.float32))
    first, second = marks
    extra = jnp.where(first, high, jnp.where(second, low, jnp.zeros_like(high)))
    return jnp.concatenate([gate, up, extra], axis=1)


def activate(total):
    units = (total.shape[1] - LANES) // 2
    sums = total[:, 2 * units : 2 * units + 1] + total[:, 2 * units + 1 : 2 * units + 2]
    scale = lax.rsqrt(sums / D + epsilon) * (1.0 / SHRINK)
    gate = total[:, :units] * scale
    up = total[:, units : 2 * units] * scale
    return narrow(jax.nn.silu(gate) * up)


def down_product(hidden, weights):
    return narrow(jnp.dot(hidden, weights[2], preferred_element_type=jnp.float32))


def shards(draft_in, verify_in, accept_len, norm_gain, gate_weight, up_weight, down_weight):
    weights = (gate_weight, up_weight, down_weight)
    n_draft, width = draft_in.shape
    n_verify = verify_in.shape[0]
    units = gate_weight.shape[1]
    all_draft = N_CHIPS * n_draft
    y = lax.axis_index("y")
    near, across, far = y % 2 == 1, lax.axis_index("xh") == 1, y // 2 == 1
    chip = lax.axis_index("xl") * SIZES["z"] + lax.axis_index("z")
    lane = lax.broadcasted_iota(jnp.int32, (1, LANES), 1)
    near, column, lane = lax.optimization_barrier((near, chip * LANES, lane))
    marks = lane == 0, lane == 1
    always = column >= 0
    mine = (lax.broadcasted_iota(jnp.int32, (1, width), 1) // LANES) == chip

    def part(body, *operands):
        def empty(*rest):
            return jax.tree.map(
                lambda a: jnp.zeros(a.shape, a.dtype), jax.eval_shape(body, *rest)
            )

        return lax.cond(always, body, empty, *operands)

    def beside(send, swaps, body, *operands):
        send, operands = lax.optimization_barrier((send, operands))
        arrived = [swap(send, axes, distance) for axes, distance in swaps]
        result = part(body, *operands)
        return lax.optimization_barrier((*arrived, result))

    def add(keep, arrived):
        return wide(keep) + wide(arrived)

    def first_rows(draft, gain, marks):
        draft = spread(draft, CHIPS, N_CHIPS)
        draft, gain = lax.optimization_barrier((draft, gain))
        draft = draft.reshape(all_draft, width)
        own = rearrange(copy_kernel, (draft,), draft.shape, "own", LOAD)
        start = (0, column)
        state = lax.dynamic_slice(
            draft, start, (all_draft, LANES), allow_negative_indices=False
        )
        return up_product(pair(own, "c", 1), gain, marks, weights), state

    def rows_in(state, gain, marks):
        own = columns(spread(state, CHIPS, N_CHIPS))
        return up_product(pair(own, "c", 1), gain, marks, weights)

    def sum_width(packet):
        packet = packet.reshape(N_GX, -1, packet.shape[1])
        return activate(summed(exchange(packet, GX)))

    def share_hidden(hidden):
        hidden = spread(hidden, GX, N_GX).reshape(-1, units)
        keep, send = halves(down_product(hidden, weights))
        return narrow(add(keep, swap(send, "c", 1)))

    def share_first(hidden, verify, gain, marks):
        hidden = spread(hidden, GX, N_GX).reshape(-1, units)
        hidden, verify, gain = lax.optimization_barrier((hidden, verify, gain))
        keep, send = halves(down_product(hidden, weights))
        partial = narrow(add(keep, swap(send, "c", 1)))
        own = up_product(verify, gain, marks, weights)
        other = up_product(swap(verify, "c", 1), gain, marks, weights)
        return partial, jnp.where(near, other, own), jnp.where(near, own, other)

    def share_both(hidden, verify):
        n_own = hidden.shape[0]
        both = spread(jnp.concatenate([hidden, verify], axis=0), GX, N_GX)
        hidden = both[:, :n_own].reshape(-1, units)
        keep, send = halves(down_product(hidden, weights))
        partial = narrow(add(keep, swap(send, "c", 1)))
        verify = both[:, n_own:].reshape(2, 2, 2, 2, 2, n_verify, units)
        verify = jnp.transpose(verify, (1, 2, 0, 4, 3, 5, 6)).reshape(-1, units)
        return partial, *halves(down_product(verify, weights))

    def share_last(hidden, state):
        hidden = spread(hidden, GX, N_GX).reshape(-1, units)
        keep, send = halves(down_product(hidden, weights))
        total = add(keep, swap(send, "c", 1))
        return narrow(total + jnp.where(mine, jnp.tile(wide(state), (1, N_CHIPS)), 0.0))

    def sum_units(partial, state):
        change = summed(exchange(blocks_of(partial, N_CHIPS), CHIPS))
        return narrow(wide(state) + change)

    def last_sum(partial):
        return narrow(summed(exchange(partial.reshape(N_CHIPS, n_draft, width), CHIPS)))

    swaps = [("z", 4), ("z", 2), ("z", 6)]
    far_z, near_z, both_z, (packet, state) = beside(
        verify_in, swaps, first_rows, draft_in, norm_gain, marks
    )
    verify = stack(verify_in, near_z, far_z, both_z)
    swaps = [(CHIPS, 1), (CHIPS, 8), (CHIPS, 9)]
    near_z, low_x, both, hidden = beside(verify, swaps, sum_width, packet)
    verify = stack(verify, near_z, low_x, both)
    partial, keep, send = part(share_first, hidden, verify, norm_gain, marks)
    arrived, state = beside(send, [("y", 1)], sum_units, partial, state)
    keep, send = halves(narrow(add(keep, arrived)), across)
    arrived, packet = beside(send, [("xh", 1)], rows_in, state, norm_gain, marks)
    keep, send = halves(narrow(add(keep, arrived)), far)
    arrived, hidden = beside(send, [("y", 2)], sum_width, packet)
    verify = activate(add(keep, arrived))
    partial, keep, send = part(share_both, hidden, verify)
    arrived, state = beside(send, [("c", 1)], sum_units, partial, state)
    keep, send = halves(narrow(add(keep, arrived)))
    arrived, packet = beside(send, [("xl", 1)], rows_in, state, norm_gain, marks)
    keep, send = halves(narrow(add(keep, arrived)))
    arrived, hidden = beside(send, [("z", 1)], sum_width, packet)
    keep, send = halves(narrow(add(keep, arrived)))
    arrived, partial = beside(send, [("z", 2)], share_last, hidden, state)
    keep, send = halves(narrow(add(keep, arrived)))
    arrived, draft_out = beside(send, [("z", 4)], last_sum, partial)
    live = (
        (jnp.arange(POS, dtype=jnp.int32)[None, :] <= accept_len[:, None])
        .reshape(-1, 1)
        .astype(jnp.float32)
    )
    verify_out = narrow(wide(verify_in) + live * add(keep, arrived))
    return draft_out, verify_out


def solution(mesh):
    split = Mesh(mesh.devices.reshape(tuple(SIZES.values())), NAMES)
    gy = ("xl", "z", "c")
    placed = (P(gy, GX), P(gy, GX), P(gy), P(GX), P(GX, gy), P(GX, gy), P(gy, GX))
    return jax.shard_map(
        shards,
        mesh=split,
        in_specs=placed,
        out_specs=(P(gy, GX), P(gy, GX)),
        check_vma=False,
    )
```

```python
import math

import jax
import jax.numpy as jnp
from jax import lax
from jax.experimental import pallas as pl
from jax.experimental.pallas import tpu as pltpu
from jax.sharding import Mesh
from jax.sharding import PartitionSpec as P

D = 16384
DRAFT_STEPS = 3
POS = 4
SIZES = {"y": 4, "xh": 2, "xl": 2, "z": 8, "c": 2}
NAMES = tuple(SIZES)
GX = ("y", "xh")
CHIPS = ("xl", "z")
N_GX = 8
N_CHIPS = 16
LANES = 128
LOAD = 32 << 20
epsilon = 1e-05
SHRINK = 2.0**-12


def swap(x, axes, distance):
    count = math.prod(SIZES[axis] for axis in ([axes] if isinstance(axes, str) else axes))
    return lax.ppermute(x, axes, [(i, i ^ distance) for i in range(count)])


def exchange(x, axes):
    return lax.all_to_all(x, axes, 0, 0)


def repeat_kernel(x, out):
    values = x[...]
    for i in range(out.shape[0]):
        out[i] = values


def stack_kernel(*refs):
    rows = [ref[...].astype(jnp.float32) for ref in refs[:-1]]
    refs[-1][...] = jnp.concatenate(rows, axis=0).astype(refs[-1].dtype)


def copy_kernel(x, out):
    out[...] = x[...]


def columns_kernel(blocks, out):
    size = blocks.shape[2]
    for k in range(blocks.shape[0]):
        out[:, k * size : (k + 1) * size] = blocks[k]


def rearrange(kernel, arrays, shape, name, load=0):
    vmem = pl.BlockSpec(memory_space=pltpu.VMEM)
    return pl.pallas_call(
        kernel,
        out_shape=jax.ShapeDtypeStruct(shape, jnp.bfloat16),
        in_specs=[vmem] * len(arrays),
        out_specs=vmem,
        compiler_params=pltpu.CompilerParams(vmem_limit_bytes=8 << 20),
        cost_estimate=pl.CostEstimate(
            flops=load * 600, bytes_accessed=4 * math.prod(shape) + load, transcendentals=0
        ),
        name=name,
    )(*arrays)


def stack(*arrays):
    count, width = arrays[0].shape
    return rearrange(stack_kernel, arrays, (len(arrays) * count, width), "stack")


def spread(x, axes, count):
    copies = rearrange(repeat_kernel, (x,), (count,) + x.shape, "repeat", LOAD)
    return exchange(copies, axes)


def wide(x):
    return x.astype(jnp.float32)


def narrow(x):
    return x.astype(jnp.bfloat16)


def pair(own, axis, distance):
    return jnp.concatenate([own, swap(own, axis, distance)], axis=0)


def halves(rows, upper=None):
    half = rows.shape[0] // 2
    low, high = rows[:half], rows[half:]
    if upper is None:
        return low, high
    return jnp.where(upper, high, low), jnp.where(upper, low, high)


def columns(blocks):
    count, rows, lanes = blocks.shape
    return rearrange(columns_kernel, (blocks,), (rows, count * lanes), "columns")


def blocks_of(x, count):
    return jnp.transpose(x.reshape(x.shape[0], count, -1), (1, 0, 2))


def summed(packet):
    return jnp.sum(wide(packet), axis=0)


def up_product(rows, gain, marks, weights):
    gate_weight, up_weight = weights[:2]
    values = wide(rows)
    squares = jnp.sum(values * values, axis=1, keepdims=True)
    high = narrow(squares)
    rest = squares - wide(high)
    low = narrow(jnp.where(jnp.isfinite(rest), rest, 0.0))
    scaled = narrow(values * SHRINK * wide(gain))
    gate = narrow(jnp.dot(scaled, gate_weight, preferred_element_type=jnp.float32))
    up = narrow(jnp.dot(scaled, up_weight, preferred_element_type=jnp.float32))
    first, second = marks
    extra = jnp.where(first, high, jnp.where(second, low, jnp.zeros_like(high)))
    return jnp.concatenate([gate, up, extra], axis=1)


def activate(total):
    units = (total.shape[1] - LANES) // 2
    sums = total[:, 2 * units : 2 * units + 1] + total[:, 2 * units + 1 : 2 * units + 2]
    scale = lax.rsqrt(sums / D + epsilon) * (1.0 / SHRINK)
    gate = total[:, :units] * scale
    up = total[:, units : 2 * units] * scale
    return narrow(jax.nn.silu(gate) * up)


def down_product(hidden, weights):
    return narrow(jnp.dot(hidden, weights[2], preferred_element_type=jnp.float32))


def shards(draft_in, verify_in, accept_len, norm_gain, gate_weight, up_weight, down_weight):
    weights = (gate_weight, up_weight, down_weight)
    n_draft, width = draft_in.shape
    n_verify = verify_in.shape[0]
    units = gate_weight.shape[1]
    all_draft = N_CHIPS * n_draft
    y = lax.axis_index("y")
    near, across, far = y % 2 == 1, lax.axis_index("xh") == 1, y // 2 == 1
    chip = lax.axis_index("xl") * SIZES["z"] + lax.axis_index("z")
    lane = lax.broadcasted_iota(jnp.int32, (1, LANES), 1)
    near, column, lane = lax.optimization_barrier((near, chip * LANES, lane))
    marks = lane == 0, lane == 1
    always = column >= 0
    mine = (lax.broadcasted_iota(jnp.int32, (1, width), 1) // LANES) == chip

    def part(body, *operands):
        def empty(*rest):
            return jax.tree.map(
                lambda a: jnp.zeros(a.shape, a.dtype), jax.eval_shape(body, *rest)
            )

        return lax.cond(always, body, empty, *operands)

    def beside(send, swaps, body, *operands):
        send, operands = lax.optimization_barrier((send, operands))
        arrived = [swap(send, axes, distance) for axes, distance in swaps]
        result = part(body, *operands)
        return lax.optimization_barrier((*arrived, result))

    def add(keep, arrived):
        return wide(keep) + wide(arrived)

    def first_rows(draft, gain, marks):
        draft = exchange(draft, CHIPS)
        draft, gain = lax.optimization_barrier((draft, gain))
        draft = draft.reshape(all_draft, width)
        own = rearrange(copy_kernel, (draft,), draft.shape, "own", LOAD)
        start = (0, column)
        state = lax.dynamic_slice(
            draft, start, (all_draft, LANES), allow_negative_indices=False
        )
        return up_product(pair(own, "c", 1), gain, marks, weights), state

    def rows_in(state, gain, marks):
        own = columns(spread(state, CHIPS, N_CHIPS))
        return up_product(pair(own, "c", 1), gain, marks, weights)

    def sum_width(packet):
        packet = packet.reshape(N_GX, -1, packet.shape[1])
        return activate(summed(exchange(packet, GX)))

    def share_hidden(hidden):
        hidden = spread(hidden, GX, N_GX).reshape(-1, units)
        keep, send = halves(down_product(hidden, weights))
        return narrow(add(keep, swap(send, "c", 1)))

    def share_first(hidden, verify, gain, marks):
        hidden = spread(hidden, GX, N_GX).reshape(-1, units)
        hidden, verify, gain = lax.optimization_barrier((hidden, verify, gain))
        keep, send = halves(down_product(hidden, weights))
        partial = narrow(add(keep, swap(send, "c", 1)))
        own = up_product(verify, gain, marks, weights)
        partial, other = lax.optimization_barrier((partial, swap(verify, "c", 1)))
        other = up_product(other, gain, marks, weights)
        return partial, jnp.where(near, other, own), jnp.where(near, own, other)

    def share_both(hidden, verify):
        n_own = hidden.shape[0]
        both = spread(jnp.concatenate([hidden, verify], axis=0), GX, N_GX)
        hidden = both[:, :n_own].reshape(-1, units)
        keep, send = halves(down_product(hidden, weights))
        partial = narrow(add(keep, swap(send, "c", 1)))
        verify = both[:, n_own:].reshape(2, 2, 2, 2, 2, n_verify, units)
        verify = jnp.transpose(verify, (1, 2, 0, 4, 3, 5, 6)).reshape(-1, units)
        return partial, *halves(down_product(verify, weights))

    def share_last(hidden, state):
        hidden = spread(hidden, GX, N_GX).reshape(-1, units)
        keep, send = halves(down_product(hidden, weights))
        total = add(keep, swap(send, "c", 1))
        return narrow(total + jnp.where(mine, jnp.tile(wide(state), (1, N_CHIPS)), 0.0))

    def sum_units(partial, state):
        change = summed(exchange(blocks_of(partial, N_CHIPS), CHIPS))
        return narrow(wide(state) + change)

    def last_sum(partial):
        return narrow(summed(exchange(partial.reshape(N_CHIPS, n_draft, width), CHIPS)))

    swaps = [("z", 4), ("z", 2), ("z", 6)]
    copies = rearrange(repeat_kernel, (draft_in,), (N_CHIPS,) + draft_in.shape, "repeat")
    far_z, near_z, both_z, (packet, state) = beside(
        verify_in, swaps, first_rows, copies, norm_gain, marks
    )
    verify = stack(verify_in, near_z, far_z, both_z)
    swaps = [(CHIPS, 1), (CHIPS, 8), (CHIPS, 9)]
    near_z, low_x, both, hidden = beside(verify, swaps, sum_width, packet)
    verify = stack(verify, near_z, low_x, both)
    partial, keep, send = part(share_first, hidden, verify, norm_gain, marks)
    arrived, state = beside(send, [("y", 1)], sum_units, partial, state)
    keep, send = halves(narrow(add(keep, arrived)), across)
    arrived, packet = beside(send, [("xh", 1)], rows_in, state, norm_gain, marks)
    keep, send = halves(narrow(add(keep, arrived)), far)
    arrived, hidden = beside(send, [("y", 2)], sum_width, packet)
    verify = activate(add(keep, arrived))
    partial, keep, send = part(share_both, hidden, verify)
    arrived, state = beside(send, [("c", 1)], sum_units, partial, state)
    keep, send = halves(narrow(add(keep, arrived)))
    arrived, packet = beside(send, [("xl", 1)], rows_in, state, norm_gain, marks)
    keep, send = halves(narrow(add(keep, arrived)))
    arrived, hidden = beside(send, [("z", 1)], sum_width, packet)
    keep, send = halves(narrow(add(keep, arrived)))
    arrived, partial = beside(send, [("z", 2)], share_last, hidden, state)
    keep, send = halves(narrow(add(keep, arrived)))
    arrived, draft_out = beside(send, [("z", 4)], last_sum, partial)
    live = (
        (jnp.arange(POS, dtype=jnp.int32)[None, :] <= accept_len[:, None])
        .reshape(-1, 1)
        .astype(jnp.float32)
    )
    verify_out = narrow(wide(verify_in) + live * add(keep, arrived))
    return draft_out, verify_out


def solution(mesh):
    split = Mesh(mesh.devices.reshape(tuple(SIZES.values())), NAMES)
    gy = ("xl", "z", "c")
    placed = (P(gy, GX), P(gy, GX), P(gy), P(GX), P(GX, gy), P(GX, gy), P(gy, GX))
    return jax.shard_map(
        shards,
        mesh=split,
        in_specs=placed,
        out_specs=(P(gy, GX), P(gy, GX)),
        check_vma=False,
    )
```

```python
import math

import jax
import jax.numpy as jnp
from jax import lax
from jax.experimental import pallas as pl
from jax.experimental.pallas import tpu as pltpu
from jax.sharding import Mesh
from jax.sharding import PartitionSpec as P

D = 16384
DRAFT_STEPS = 3
POS = 4
SIZES = {"y": 4, "xh": 2, "xl": 2, "z": 8, "c": 2}
NAMES = tuple(SIZES)
GX = ("y", "xh")
CHIPS = ("xl", "z")
N_GX = 8
N_CHIPS = 16
LANES = 128
LOAD = 32 << 20
epsilon = 1e-05
SHRINK = 2.0**-12


def swap(x, axes, distance):
    count = math.prod(SIZES[axis] for axis in ([axes] if isinstance(axes, str) else axes))
    return lax.ppermute(x, axes, [(i, i ^ distance) for i in range(count)])


def exchange(x, axes):
    return lax.all_to_all(x, axes, 0, 0)


def repeat_kernel(x, out):
    values = x[...]
    for i in range(out.shape[0]):
        out[i] = values


def stack_kernel(*refs):
    rows = [ref[...].astype(jnp.float32) for ref in refs[:-1]]
    refs[-1][...] = jnp.concatenate(rows, axis=0).astype(refs[-1].dtype)


def copy_kernel(x, out):
    out[...] = x[...]


def columns_kernel(blocks, out):
    size = blocks.shape[2]
    for k in range(blocks.shape[0]):
        out[:, k * size : (k + 1) * size] = blocks[k]


def rearrange(kernel, arrays, shape, name, load=0):
    vmem = pl.BlockSpec(memory_space=pltpu.VMEM)
    return pl.pallas_call(
        kernel,
        out_shape=jax.ShapeDtypeStruct(shape, jnp.bfloat16),
        in_specs=[vmem] * len(arrays),
        out_specs=vmem,
        compiler_params=pltpu.CompilerParams(vmem_limit_bytes=8 << 20),
        cost_estimate=pl.CostEstimate(
            flops=load * 600, bytes_accessed=4 * math.prod(shape) + load, transcendentals=0
        ),
        name=name,
    )(*arrays)


def stack(*arrays):
    count, width = arrays[0].shape
    return rearrange(stack_kernel, arrays, (len(arrays) * count, width), "stack")


def spread(x, axes, count):
    copies = rearrange(repeat_kernel, (x,), (count,) + x.shape, "repeat", LOAD)
    return exchange(copies, axes)


def wide(x):
    return x.astype(jnp.float32)


def narrow(x):
    return x.astype(jnp.bfloat16)


def pair(own, axis, distance):
    return jnp.concatenate([own, swap(own, axis, distance)], axis=0)


def halves(rows, upper=None):
    half = rows.shape[0] // 2
    low, high = rows[:half], rows[half:]
    if upper is None:
        return low, high
    return jnp.where(upper, high, low), jnp.where(upper, low, high)


def columns(blocks):
    count, rows, lanes = blocks.shape
    return rearrange(columns_kernel, (blocks,), (rows, count * lanes), "columns")


def blocks_of(x, count):
    return jnp.transpose(x.reshape(x.shape[0], count, -1), (1, 0, 2))


def summed(packet):
    return jnp.sum(wide(packet), axis=0)


def up_product(rows, gain, marks, weights):
    gate_weight, up_weight = weights[:2]
    values = wide(rows)
    squares = jnp.sum(values * values, axis=1, keepdims=True)
    high = narrow(squares)
    rest = squares - wide(high)
    low = narrow(jnp.where(jnp.isfinite(rest), rest, 0.0))
    scaled = narrow(values * SHRINK * wide(gain))
    gate = narrow(jnp.dot(scaled, gate_weight, preferred_element_type=jnp.float32))
    up = narrow(jnp.dot(scaled, up_weight, preferred_element_type=jnp.float32))
    first, second = marks
    extra = jnp.where(first, high, jnp.where(second, low, jnp.zeros_like(high)))
    return jnp.concatenate([gate, up, extra], axis=1)


def activate(total):
    units = (total.shape[1] - LANES) // 2
    sums = total[:, 2 * units : 2 * units + 1] + total[:, 2 * units + 1 : 2 * units + 2]
    scale = lax.rsqrt(sums / D + epsilon) * (1.0 / SHRINK)
    gate = total[:, :units] * scale
    up = total[:, units : 2 * units] * scale
    return narrow(jax.nn.silu(gate) * up)


def down_product(hidden, weights):
    return narrow(jnp.dot(hidden, weights[2], preferred_element_type=jnp.float32))


def shards(draft_in, verify_in, accept_len, norm_gain, gate_weight, up_weight, down_weight):
    weights = (gate_weight, up_weight, down_weight)
    n_draft, width = draft_in.shape
    n_verify = verify_in.shape[0]
    units = gate_weight.shape[1]
    all_draft = N_CHIPS * n_draft
    y = lax.axis_index("y")
    near, across, far = y % 2 == 1, lax.axis_index("xh") == 1, y // 2 == 1
    chip = lax.axis_index("xl") * SIZES["z"] + lax.axis_index("z")
    lane = lax.broadcasted_iota(jnp.int32, (1, LANES), 1)
    near, column, lane = lax.optimization_barrier((near, chip * LANES, lane))
    marks = lane == 0, lane == 1
    always = column >= 0
    mine = (lax.broadcasted_iota(jnp.int32, (1, width), 1) // LANES) == chip

    def part(body, *operands):
        def empty(*rest):
            return jax.tree.map(
                lambda a: jnp.zeros(a.shape, a.dtype), jax.eval_shape(body, *rest)
            )

        return lax.cond(always, body, empty, *operands)

    def beside(send, swaps, body, *operands):
        send, operands = lax.optimization_barrier((send, operands))
        arrived = [swap(send, axes, distance) for axes, distance in swaps]
        result = part(body, *operands)
        return lax.optimization_barrier((*arrived, result))

    def add(keep, arrived):
        return wide(keep) + wide(arrived)

    def first_rows(draft, gain, marks):
        draft = exchange(draft, CHIPS)
        draft, gain = lax.optimization_barrier((draft, gain))
        draft = draft.reshape(all_draft, width)
        own = rearrange(copy_kernel, (draft,), draft.shape, "own", LOAD)
        start = (0, column)
        state = lax.dynamic_slice(
            draft, start, (all_draft, LANES), allow_negative_indices=False
        )
        return up_product(pair(own, "c", 1), gain, marks, weights), state

    def rows_in(state, gain, marks):
        own = columns(spread(state, CHIPS, N_CHIPS))
        return up_product(pair(own, "c", 1), gain, marks, weights)

    def sum_width(packet):
        packet = packet.reshape(N_GX, -1, packet.shape[1])
        return activate(summed(exchange(packet, GX)))

    def share_hidden(hidden):
        hidden = spread(hidden, GX, N_GX).reshape(-1, units)
        keep, send = halves(down_product(hidden, weights))
        return narrow(add(keep, swap(send, "c", 1)))

    def share_first(hidden, verify, gain, marks):
        hidden = spread(hidden, GX, N_GX).reshape(-1, units)
        hidden, verify, gain = lax.optimization_barrier((hidden, verify, gain))
        keep, send = halves(down_product(hidden, weights))
        partial = narrow(add(keep, swap(send, "c", 1)))
        own = up_product(verify, gain, marks, weights)
        partial, other = lax.optimization_barrier((partial, swap(verify, "c", 1)))
        other = up_product(other, gain, marks, weights)
        return partial, jnp.where(near, other, own), jnp.where(near, own, other)

    def share_both(hidden, verify):
        n_own = hidden.shape[0]
        both = spread(jnp.concatenate([hidden, verify], axis=0), GX, N_GX)
        hidden = both[:, :n_own].reshape(-1, units)
        keep, send = halves(down_product(hidden, weights))
        partial = narrow(add(keep, swap(send, "c", 1)))
        verify = both[:, n_own:].reshape(2, 2, 2, 2, 2, n_verify, units)
        verify = jnp.transpose(verify, (1, 2, 0, 3, 4, 5, 6)).reshape(-1, units)
        return partial, *halves(down_product(verify, weights))

    def share_last(hidden, state):
        hidden = spread(hidden, GX, N_GX).reshape(-1, units)
        keep, send = halves(down_product(hidden, weights))
        total = add(keep, swap(send, "c", 1))
        return narrow(total + jnp.where(mine, jnp.tile(wide(state), (1, N_CHIPS)), 0.0))

    def sum_units(partial, state):
        change = summed(exchange(blocks_of(partial, N_CHIPS), CHIPS))
        return narrow(wide(state) + change)

    def last_sum(partial):
        return narrow(summed(exchange(partial.reshape(N_CHIPS, n_draft, width), CHIPS)))

    swaps = [("z", 4), ("z", 2), ("z", 6)]
    copies = rearrange(repeat_kernel, (draft_in,), (N_CHIPS,) + draft_in.shape, "repeat")
    far_z, near_z, both_z, (packet, state) = beside(
        verify_in, swaps, first_rows, copies, norm_gain, marks
    )
    verify = stack(verify_in, near_z, far_z, both_z)
    swaps = [(CHIPS, 1), (CHIPS, 8), (CHIPS, 9)]
    near_z, low_x, both, hidden = beside(verify, swaps, sum_width, packet)
    verify = stack(verify, near_z, low_x, both)
    partial, keep, send = part(share_first, hidden, verify, norm_gain, marks)
    arrived, state = beside(send, [("y", 1)], sum_units, partial, state)
    keep, send = halves(narrow(add(keep, arrived)), across)
    arrived, packet = beside(send, [("xh", 1)], rows_in, state, norm_gain, marks)
    keep, send = halves(narrow(add(keep, arrived)), far)
    arrived, hidden = beside(send, [("y", 2)], sum_width, packet)
    verify = activate(add(keep, arrived))
    partial, keep, send = part(share_both, hidden, verify)
    arrived, state = beside(send, [("c", 1)], sum_units, partial, state)
    keep, send = halves(narrow(add(keep, arrived)))
    arrived, packet = beside(send, [("xl", 1)], rows_in, state, norm_gain, marks)
    keep, send = halves(narrow(add(keep, arrived)))
    arrived, hidden = beside(send, [("z", 1)], sum_width, packet)
    keep, send = halves(narrow(add(keep, arrived)))
    arrived, partial = beside(send, [("z", 4)], share_last, hidden, state)
    keep, send = halves(narrow(add(keep, arrived)))
    arrived, draft_out = beside(send, [("z", 2)], last_sum, partial)
    live = (
        (jnp.arange(POS, dtype=jnp.int32)[None, :] <= accept_len[:, None])
        .reshape(-1, 1)
        .astype(jnp.float32)
    )
    verify_out = narrow(wide(verify_in) + live * add(keep, arrived))
    return draft_out, verify_out


def solution(mesh):
    split = Mesh(mesh.devices.reshape(tuple(SIZES.values())), NAMES)
    gy = ("xl", "z", "c")
    placed = (P(gy, GX), P(gy, GX), P(gy), P(GX), P(GX, gy), P(GX, gy), P(gy, GX))
    return jax.shard_map(
        shards,
        mesh=split,
        in_specs=placed,
        out_specs=(P(gy, GX), P(gy, GX)),
        check_vma=False,
    )
```
